128 devices in a mesh: row: 16 (over y, x), col: 8 (over z, core).
Axes of the slice: x: 4, y: 4, z: 4, core: 2. Of those that a mesh axis runs over, the one named last changes fastest.
Arguments:
- occ_coef: bfloat16 [1024, 16384], P('row', 'col'), may hold values from -6 to 6
- vir_coef: bfloat16 [2048, 16384], P('row', 'col'), may hold values from -6 to 6
- atom_counts: int32 [8, 768], P('col'), may hold values from 1 to 9, 2048 in all within a row
- occ_index: int32 [1024], P('row'), may hold values from 0 to 1023
- vir_index: int32 [1024], P('row'), may hold values from 0 to 2047
- interaction: bfloat16 [6144, 6144], P('col', 'row'), as said below
- window_charges: bfloat16 [131072, 6144], P(('row', 'col')), may hold values from -0.078125 to 0.078125
- panel_start: int32 [1], replicated, may hold values from 0 to 130048
Outputs:
- coupling: bfloat16 [1024, 131072], P(None, ('row', 'col'))
The draws below stay inside these ranges and needn't reach their ends.
Inputs may be any that keep to these rules, and one draw needn't show every extreme that they name: Each line of atom_counts sums to 2048. interaction is symmetric, with its diagonal between 0.5 and 1.5.
All inputs are finite; a program needn't handle non-finite values.
Results may differ from the reference program's by a relative error of at most 0.017.
Values may be sent and summed in bfloat16 or wider, within the bound.
A program may use at most 128 MiB of HBM per device.

```python
import math
import jax
import jax.numpy as jnp
import numpy as np
from jax import lax

NATOM = 6144
NBF = 16384
MOST_BF = 9
NOCC = 1024
NVIR = 2048
NPANEL = 1024
WIN_DEV = 1024
NWIN = 131072
ATOM_DEV = 768
BF_DEV = 2048
COL_BLOCKS = 8


def draw_interaction(key, part):
    key = jax.random.fold_in(key, 11)
    first_key, second_key = jax.random.split(key, 2)
    raw_values = jax.random.normal(first_key, (NATOM, NATOM), jnp.float32)
    off_diagonal = (raw_values + raw_values.T) * (0.70710678 / NATOM ** 0.5)
    hardness = jax.random.uniform(second_key, (NATOM,), jnp.float32, 0.5, 1.5)
    row_index = lax.broadcasted_iota(jnp.int32, (NATOM, NATOM), 0)
    col_index = lax.broadcasted_iota(jnp.int32, (NATOM, NATOM), 1)
    return jnp.where(row_index == col_index, hardness[:, None] + jnp.zeros_like(off_diagonal), off_diagonal).astype(jnp.bfloat16)


def plant(entries, key, smallest, top_value):
    longest = entries.shape.index(max(entries.shape))
    spots = []
    for shift in (0, 1):
        where = [jax.random.randint(jax.random.fold_in(key, axis), (), 0, length) for axis, length in enumerate(entries.shape)]
        where[longest] = (where[longest] + shift) % entries.shape[longest]
        spots.append(tuple(where))
    return entries.at[spots[0]].set(smallest).at[spots[1]].set(top_value)


def shard_levels(key, dims, pieces, low, largest):
    gain = 1.0
    for dim, blocks in pieces:
        steps = jax.random.uniform(jax.random.fold_in(jax.random.fold_in(key, 6), dim), (blocks,), jnp.float32, low / len(pieces), largest / len(pieces))
        gain = gain * jnp.repeat(jnp.exp(steps), dims[dim] // blocks).reshape((-1,) + (1,) * (len(dims) - 1 - dim))
    return gain


def split_up(count, total, reach, lean):
    weights = [(1 << 20) // math.isqrt(grade ** lean) + 1 for grade in range(2, count + 1)]
    rest, given = total - reach - (count - 1), [1] * (count - 1)
    while rest > 0:
        movable = [i for i in range(count - 1) if given[i] < reach]
        pool, remaining = sum([weights[i] for i in movable]), rest
        for i in movable:
            more = min(reach - given[i], max(1, remaining * weights[i] // pool), rest)
            given[i] = given[i] + more
            rest = rest - more
    return np.array([reach] + given)


def uneven_parts(stream_key, amount, total, most, lean):
    if amount == 2:
        one = jax.random.randint(stream_key, (), max(1, total - most), min(most, total - 1) + 1)
        return jnp.stack([one, total - one])
    lengths = jnp.asarray(split_up(amount, total, most, lean), jnp.int32)
    pairs = (amount - 1) // 2
    donor, sink = lengths[1:1 + 2 * pairs:2], lengths[2:2 + 2 * pairs:2]
    margin = jnp.minimum(donor - 1, most - sink)
    moved = jax.random.randint(jax.random.fold_in(stream_key, 1), (pairs,), 0, 1 << 20) % (margin + 1)
    lengths = lengths.at[1:1 + 2 * pairs:2].set(donor - moved).at[2:2 + 2 * pairs:2].set(sink + moved)
    return lengths[jax.random.permutation(jax.random.fold_in(stream_key, 2), amount)]


def noise(key, shape, deviation, bound, cuts=(), kind=jnp.bfloat16):
    level = shard_levels(key, shape, cuts, -0.22, 0.18) if cuts else 1.0
    values = jax.random.normal(key, shape, jnp.float32) * deviation * level
    return jnp.minimum(jnp.maximum(values, -bound), bound).astype(kind)


def setup_inputs(seed: int = 0) -> dict:
    key_list = jax.random.split(jax.random.key(seed), 9)
    occ_coef = noise(key_list[0], (NOCC, NBF), 1.0, 6.0, ((0, 16), (1, 8)))
    vir_coef = noise(key_list[1], (NVIR, NBF), 1.0, 6.0, ((0, 16), (1, 8)))
    atom_counts = jax.vmap(lambda own: uneven_parts(own, ATOM_DEV, BF_DEV, MOST_BF, 0))(jax.random.split(key_list[2], COL_BLOCKS)).reshape((COL_BLOCKS, ATOM_DEV)).astype(jnp.int32)
    occ_index = plant(jax.random.randint(key_list[3], (NPANEL,), 0, NOCC), jax.random.fold_in(key_list[3], 1), 0, NOCC - 1).astype(jnp.int32)
    vir_index = plant(jax.random.randint(key_list[4], (NPANEL,), 0, NVIR), jax.random.fold_in(key_list[4], 1), 0, NVIR - 1).astype(jnp.int32)
    interaction = draw_interaction(jax.random.fold_in(key_list[8], 71), 0)
    window_charges = noise(key_list[6], (NWIN, NATOM), NATOM ** -0.5, 0.078125, ((0, 128),))
    panel_start = jax.random.randint(key_list[7], (1,), 0, NWIN - NPANEL + 1).astype(jnp.int32)
    return {"occ_coef": occ_coef, "vir_coef": vir_coef, "atom_counts": atom_counts, "occ_index": occ_index, "vir_index": vir_index, "interaction": interaction, "window_charges": window_charges, "panel_start": panel_start}


def reference(occ_coef, vir_coef, atom_counts, occ_index, vir_index, interaction, window_charges, panel_start):
    counts = atom_counts.reshape(-1)
    atom_owner = jnp.repeat(jnp.arange(NATOM, dtype=jnp.int32), counts, total_repeat_length=NBF)
    density = occ_coef[occ_index].astype(jnp.float32) * vir_coef[vir_index].astype(jnp.float32)
    charges = jax.ops.segment_sum(density.T, atom_owner, num_segments=NATOM)
    panel_charges = charges.T.astype(jnp.bfloat16)
    potential = lax.dot_general(interaction, panel_charges, (((0,), (1,)), ((), ())), preferred_element_type=jnp.float32).astype(jnp.bfloat16)
    blocks = window_charges.reshape(NWIN // WIN_DEV, WIN_DEV, NATOM)
    panel_index = jnp.arange(NPANEL, dtype=jnp.int32)[:, None]

    def one_block(packed):
        block_id, rows_here = packed
        values = lax.dot_general(potential, rows_here, (((0,), (1,)), ((), ())), preferred_element_type=jnp.float32)
        window_index = block_id * WIN_DEV + jnp.arange(WIN_DEV, dtype=jnp.int32)[None, :]
        return jnp.where(window_index >= panel_start[0] + panel_index, values, jnp.zeros_like(values)).astype(jnp.bfloat16)

    result = lax.map(one_block, (jnp.arange(NWIN // WIN_DEV, dtype=jnp.int32), blocks))
    return jnp.transpose(result, (1, 0, 2)).reshape(NPANEL, NWIN)
```

```python
import jax
import jax.numpy as jnp
from jax import lax
from jax.experimental import pallas as pl
from jax.experimental.pallas import tpu as pltpu
from jax.sharding import PartitionSpec as P

MESH = pl.DeviceIdType.MESH
BF = jnp.bfloat16
F32 = jnp.float32


def place():
    row, col = lax.axis_index("row"), lax.axis_index("col")
    return lax.div(row, 4), lax.rem(row, 4), lax.div(col, 2), lax.rem(col, 2)


def step(c, d):
    return lax.rem(c + d, 4)


def device(y, x, z, k):
    return (y * 4 + x, z * 2 + k)


def send(src, dst, send_sem, recv_sem, target):
    copy = pltpu.make_async_remote_copy(
        src_ref=src, dst_ref=dst, send_sem=send_sem, recv_sem=recv_sem, device_id=target, device_id_type=MESH
    )
    copy.start()
    return copy


def arrived(ref, send_sem, recv_sem, me):
    pltpu.make_async_remote_copy(
        src_ref=ref, dst_ref=ref, send_sem=send_sem, recv_sem=recv_sem, device_id=me, device_id_type=MESH
    ).wait_recv()


def greet(targets):
    barrier = pltpu.get_barrier_semaphore()
    for target in targets:
        pl.semaphore_signal(barrier, inc=1, device_id=target, device_id_type=MESH)
    pl.semaphore_wait(barrier, len(targets))


def iota(shape, dim):
    return lax.broadcasted_iota(jnp.int32, shape, dim).astype(F32)


def front(idx_hbm, occ_hbm, vir_hbm, counts_ref, inter_hbm, out_ref,
          idx_all, occ_t, vir_t, pick_occ, pick_vir, member, dens_out, dens, charges, inter, half_out, half_in,
          quarter_out, quarter_in,
          idx_s, idx_r, occ_s, occ_r, vir_s, vir_r, dens_s, dens_r, ag_s, ag_r, rs_s, rs_r, loc):
    y, x, z, k = place()
    me = device(y, x, z, k)
    r = y * 4 + x
    plane = [(step(y, d // 4), step(x, d % 4)) for d in range(1, 16)]
    greet(
        [device(yy, xx, z, k) for yy, xx in plane]
        + [device(y, x, step(z, d), k) for d in (1, 2, 3)]
        + [device(y, x, z, 1 - k)]
    )
    sent = []
    own = [
        pltpu.make_async_copy(idx_hbm, idx_all.at[r], idx_r.at[r]),
        pltpu.make_async_copy(occ_hbm.at[:, pl.ds(pl.multiple_of(r * 128, 128), 128)], occ_t.at[r], occ_r.at[r]),
        pltpu.make_async_copy(vir_hbm.at[:, pl.ds(pl.multiple_of(r * 128, 128), 128)], vir_t.at[r], vir_r.at[r]),
        pltpu.make_async_copy(inter_hbm, inter, loc.at[0]),
    ]
    for copy in own:
        copy.start()
    for d, (yy, xx) in enumerate(plane):
        sent.append(send(idx_hbm, idx_all.at[r], idx_s.at[d], idx_r.at[r], device(yy, xx, z, k)))
    for d, (yy, xx) in enumerate(plane):
        cols = pl.ds(pl.multiple_of((yy * 4 + xx) * 128, 128), 128)
        sent.append(send(occ_hbm.at[:, cols], occ_t.at[r], occ_s.at[d], occ_r.at[r], device(yy, xx, z, k)))
    for d, (yy, xx) in enumerate(plane):
        cols = pl.ds(pl.multiple_of((yy * 4 + xx) * 128, 128), 128)
        sent.append(send(vir_hbm.at[:, cols], vir_t.at[r], vir_s.at[d], vir_r.at[r], device(yy, xx, z, k)))
    counts = counts_ref[...].astype(F32)
    upper = (iota((768, 768), 0) <= iota((768, 768), 1)).astype(BF)
    ends = jnp.dot(jnp.broadcast_to(counts, (8, 768)).astype(BF), upper, preferred_element_type=F32)[0:1]
    starts = ends - counts

    def members(i, carry):
        basis = iota((256, 768), 0) + (i * 256).astype(F32)
        inside = jnp.logical_and(basis >= starts, basis < ends)
        member[pl.ds(pl.multiple_of(i * 256, 256), 256), :] = jnp.where(inside, 1.0, 0.0).astype(BF)
        return carry

    lax.fori_loop(0, 8, members, 0)

    for s in range(16):
        arrived(idx_all.at[s], idx_s.at[0], idx_r.at[s], me)

    def picks(s, carry):
        line = idx_all[s][0:1].astype(F32)
        mine = iota((128, 128), 0) == iota((128, 128), 1)
        column = jnp.sum(jnp.where(mine, jnp.broadcast_to(line, (128, 128)), 0.0), axis=1, keepdims=True)
        rows = pl.ds(pl.multiple_of(s * 64, 64), 64)
        pick_occ[rows, :] = jnp.where(column[0:64] == iota((64, 1024), 1), 1.0, 0.0).astype(BF)
        pick_vir[rows, :] = jnp.where(column[64:128] == iota((64, 2048), 1), 1.0, 0.0).astype(BF)
        return carry

    lax.fori_loop(0, 16, picks, 0)
    for s in range(16):
        arrived(occ_t.at[s], occ_s.at[0], occ_r.at[s], me)
    for s in range(16):
        arrived(vir_t.at[s], vir_s.at[0], vir_r.at[s], me)
    occ_rows, vir_rows = occ_t[...].reshape(1024, 128), vir_t[...].reshape(2048, 128)
    n = 0
    for dy in (1, 2, 3, 0):
        yy = step(y, dy)
        rows = pl.ds(pl.multiple_of(yy * 256, 256), 256)
        first = jnp.dot(pick_occ[rows, :], occ_rows, preferred_element_type=F32)
        second = jnp.dot(pick_vir[rows, :], vir_rows, preferred_element_type=F32)
        dens_out[pl.ds(yy * 4, 4)] = (first * second).astype(BF).reshape(4, 64, 128)
        for dx in (1, 2, 3, 0):
            xx = step(x, dx)
            other = yy * 4 + xx
            if dy == 0 and dx == 0:
                pltpu.make_async_copy(dens_out.at[r], dens.at[r], dens_r.at[r]).start()
            else:
                sent.append(send(dens_out.at[other], dens.at[r], dens_s.at[n], dens_r.at[r], device(yy, xx, z, k)))
                n += 1
    for s in range(16):
        arrived(dens.at[s], dens_s.at[0], dens_r.at[s], me)
    density = jnp.concatenate([dens[s] for s in range(16)], axis=1)
    charges[y, x] = jnp.dot(density, member[...], preferred_element_type=F32).astype(BF)
    n = [0]

    def slot():
        n[0] += 1
        return ag_s.at[n[0] - 1], ag_r.at[n[0] - 1]

    a_up, a_down = device(y, step(x, 1), z, k), device(y, step(x, 3), z, k)
    b_up, b_down = device(step(y, 1), x, z, k), device(step(y, 3), x, z, k)

    def stage(parts):
        slots = []
        for whole, half, c, up, down in parts:
            four = [slot() for _ in range(4)]
            slots.append(four)
            sent.append(send(whole(c), whole(c), *four[0], up))
            sent.append(send(whole(c), whole(c), *four[1], down))
        for (whole, half, c, up, down), four in zip(parts, slots):
            arrived(whole(step(c, 3)), *four[0], me)
            sent.append(send(half(step(c, 3), 0), half(step(c, 3), 0), *four[2], up))
            arrived(whole(step(c, 1)), *four[1], me)
            sent.append(send(half(step(c, 1), 1), half(step(c, 1), 1), *four[3], down))
        for (whole, half, c, up, down), four in zip(parts, slots):
            arrived(half(step(c, 2), 0), *four[2], me)
            arrived(half(step(c, 2), 1), *four[3], me)

    stage([
        (lambda s: charges.at[y, s, pl.ds(0, 32)], lambda s, h: charges.at[y, s, pl.ds(16 * h, 16)], x, a_up, a_down),
        (lambda s: charges.at[s, x, pl.ds(32, 32)], lambda s, h: charges.at[s, x, pl.ds(32 + 16 * h, 16)], y, b_up, b_down),
    ])
    stage([
        (lambda s: charges.at[s, :, pl.ds(0, 32)], lambda s, h: charges.at[s, pl.ds(2 * h, 2), pl.ds(0, 32)], y, b_up, b_down),
        (lambda s: charges.at[:, s, pl.ds(32, 32)], lambda s, h: charges.at[pl.ds(2 * h, 2), s, pl.ds(32, 32)], x, a_up, a_down),
    ])
    own[3].wait()
    theirs = charges[pl.ds((1 - k) * 2, 2)].reshape(512, 768)
    half_out[...] = jnp.dot(theirs, inter[...], preferred_element_type=F32)
    swap = send(half_out, half_in, rs_s.at[0], rs_r.at[0], device(y, x, z, 1 - k))
    sent.append(swap)
    mine = jnp.dot(charges[pl.ds(k * 2, 2)].reshape(512, 768), inter[...], preferred_element_type=F32)
    swap.wait_recv()
    quarter_out[...] = (mine + half_in[...]).reshape(4, 128, 384)
    for d in (1, 2, 3):
        zz = step(z, d)
        quarter_in[d, 0] = quarter_out[zz].astype(BF)
        sent.append(send(quarter_in.at[d, 0], quarter_in.at[d, 1], rs_s.at[d], rs_r.at[d], device(y, x, zz, k)))
    total = quarter_out[z]
    for d in (1, 2, 3):
        arrived(quarter_in.at[d, 1], rs_s.at[d], rs_r.at[d], me)
        total = total + quarter_in[d, 1].astype(F32)
    total = total.astype(BF)
    for j in range(3):
        out_ref[j] = total[:, 128 * j:128 * j + 128]
    for copy in sent:
        copy.wait_send()


def back(block_ref, win_hbm, out_ref, pot, win, acc, ici_s, ici_r, d2d_s, d2d_r, loc):
    y, x, z, k = place()
    me = device(y, x, z, k)

    def load(i, carry):
        cols = pl.ds(pl.multiple_of(i * 128, 128), 128)
        pltpu.make_async_copy(win_hbm.at[:, cols], win.at[i], loc.at[0]).start()
        return carry

    lax.fori_loop(0, 48, load, 0)
    ups = {"y": device(step(y, 1), x, z, k), "x": device(y, step(x, 1), z, k), "z": device(y, x, step(z, 1), k)}
    downs = {"y": device(step(y, 3), x, z, k), "x": device(y, step(x, 3), z, k), "z": device(y, x, step(z, 3), k)}
    at = {"y": y, "x": x, "z": z}
    twin = device(y, x, z, 1 - k)
    greet(list(ups.values()) + list(downs.values()) + [twin])
    sent = []

    def rows(s, kk=k, n=128, h=0):
        return pl.ds(pl.multiple_of(kk * 512 + s * 128 + h, 64), n)

    def half_rows(kk=k):
        return pl.ds(pl.multiple_of(kk * 512, 512), 512)

    mine = rows(z)
    orders = ("zyx", "xzy", "yxz")
    first = (
        lambda s, h=None: pot.at[0, y, x, rows(s) if h is None else rows(s, n=64, h=64 * h)],
        lambda s, h=None: pot.at[1, y, s, mine if h is None else rows(z, n=64, h=64 * h)],
        lambda s, h=None: pot.at[2, s, x, mine if h is None else rows(z, n=64, h=64 * h)],
    )
    second = (
        lambda s, h=None, kk=k: pot.at[0, s, x, half_rows(kk) if h is None else pl.ds(pl.multiple_of(kk * 512 + 256 * h, 256), 256)],
        lambda s, h=None, kk=k: pot.at[1, y, slice(None) if h is None else pl.ds(2 * h, 2), rows(s, kk)],
        lambda s, h=None, kk=k: pot.at[2, slice(None) if h is None else pl.ds(2 * h, 2), s, rows(z, kk)],
    )
    third = (
        lambda s, q, kk=k: pot.at[0, q, s, half_rows(kk)],
        lambda s, q, kk=k: pot.at[1, s, q, half_rows(kk)],
        lambda s, q, kk=k: pot.at[2, q, :, rows(s, kk)],
    )
    for j in range(3):
        pot[j, y, x, mine, :] = block_ref[j]

    n_ici, n_d2d = [0, 0, 0], [0, 0, 0]

    def slot(j):
        n_ici[j] += 1
        return ici_s.at[j, n_ici[j] - 1], ici_r.at[j, n_ici[j] - 1]

    def share(j, ref):
        n_d2d[j] += 1
        sems = d2d_s.at[j, n_d2d[j] - 1], d2d_r.at[j, n_d2d[j] - 1]
        sent.append(send(ref, ref, *sems, twin))
        return sems

    def ring(level, views):
        slots = []
        for j in range(3):
            c, axis = at[orders[j][level]], orders[j][level]
            four = [slot(j) for _ in range(4)]
            slots.append(four)
            sent.append(send(views[j](c), views[j](c), *four[0], ups[axis]))
            sent.append(send(views[j](c), views[j](c), *four[1], downs[axis]))
        for j in range(3):
            c, axis = at[orders[j][level]], orders[j][level]
            four = slots[j]
            below, above = step(c, 3), step(c, 1)
            arrived(views[j](below), *four[0], me)
            sent.append(send(views[j](below, 0), views[j](below, 0), *four[2], ups[axis]))
            arrived(views[j](above), *four[1], me)
            sent.append(send(views[j](above, 1), views[j](above, 1), *four[3], downs[axis]))
        for j in range(3):
            c = at[orders[j][level]]
            far = step(c, 2)
            arrived(views[j](far, 0), *slots[j][2], me)
            arrived(views[j](far, 1), *slots[j][3], me)

    ring(0, first)
    shared = []
    for j in range(3):
        c = at[orders[j][1]]
        shared.append([(share(j, second[j](c)), c)])
    ring(1, second)
    slots = []
    for j in range(3):
        c, axis = at[orders[j][2]], orders[j][2]
        slots.append([[slot(j) for _ in range(6)], [slot(j) for _ in range(6)]])
    for q in range(4):
        for j in range(3):
            c, axis = at[orders[j][2]], orders[j][2]
            sent.append(send(third[j](c, q), third[j](c, q), *slots[j][0][q], ups[axis]))
            sent.append(send(third[j](c, q), third[j](c, q), *slots[j][1][q], downs[axis]))
    for j in range(3):
        for d in (1, 2, 3):
            c = step(at[orders[j][1]], d)
            shared[j].append((share(j, second[j](c)), c))
    pltpu.make_async_copy(win, win, loc.at[0]).wait()

    started = [False]

    def cells(j, points):
        return [(j, yy, xx) for yy, xx in points]

    def add(points, row_starts, size):
        lhs = jnp.concatenate(
            [jnp.concatenate([pot[j, yy, xx, pl.ds(pl.multiple_of(s, 128), size), :] for s in row_starts], axis=0)
             if len(row_starts) > 1 else pot[j, yy, xx, pl.ds(pl.multiple_of(row_starts[0], 128), size), :]
             for j, yy, xx in points], axis=1)
        rhs = jnp.concatenate([win[(yy * 4 + xx) * 3 + j] for j, yy, xx in points], axis=1)
        value = lax.dot_general(lhs, rhs, (((1,), (1,)), ((), ())), preferred_element_type=F32)
        if not started[0]:
            acc[...] = value
            started[0] = True
            return
        for i, s in enumerate(row_starts):
            where = pl.ds(pl.multiple_of(s, 128), size)
            acc[where, :] += value[i * size:(i + 1) * size]

    whole = [0]
    both = lambda s: [s * 128, 512 + s * 128]

    def twin_done(j, n):
        for i in n:
            sems, c = shared[j][i]
            arrived(second[j](c, kk=1 - k), *sems, me)

    for j in range(3):
        twin_done(j, range(4))
    add(cells(0, [(q, x) for q in range(4)]), [0], 1024)
    late = [[None] * 4 for _ in range(3)]

    def take(q, j):
        c, axis = at[orders[j][2]], orders[j][2]
        below, above = step(c, 3), step(c, 1)
        up, down = slots[j]
        arrived(third[j](below, q), *up[q], me)
        if q < 2:
            sent.append(send(third[j](below, q), third[j](below, q), *up[4 + q], ups[axis]))
        a = share(j, third[j](below, q))
        arrived(third[j](above, q), *down[q], me)
        if q >= 2:
            sent.append(send(third[j](above, q), third[j](above, q), *down[2 + q], downs[axis]))
        b = share(j, third[j](above, q))
        return a, b

    def take_twin(q, j, sems):
        c = at[orders[j][2]]
        arrived(third[j](step(c, 3), q, 1 - k), *sems[0], me)
        arrived(third[j](step(c, 1), q, 1 - k), *sems[1], me)

    pairs = {}
    for q in range(4):
        for j in range(3):
            pairs[q, j] = take(q, j)
        if q == 0:
            add(cells(1, [(y, q) for q in range(4)]), [0], 1024)
        if q == 1:
            add(cells(2, [(a, b) for a in range(4) for b in range(4)]), both(z), 128)
        if q in (1, 3):
            for qq in (q - 1, q):
                for j in range(3):
                    take_twin(qq, j, pairs[qq, j])
            add(cells(0, [(qq, step(x, d)) for qq in (q - 1, q) for d in (1, 3)]), [0], 1024)
            add(cells(1, [(step(y, d), qq) for qq in (q - 1, q) for d in (1, 3)]), [0], 1024)
            add(cells(2, [(qq, b) for qq in (q - 1, q) for b in range(4)]), both(step(z, 1)) + both(step(z, 3)), 128)
    far = {}
    for q in range(4):
        for j in range(3):
            c = step(at[orders[j][2]], 2)
            sems = slots[j][0][4 + q] if q < 2 else slots[j][1][2 + q]
            arrived(third[j](c, q), *sems, me)
            far[q, j] = share(j, third[j](c, q))
    for j in range(3):
        for q in range(4):
            c = step(at[orders[j][2]], 2)
            arrived(third[j](c, q, 1 - k), *far[q, j], me)
    add(cells(0, [(q, step(x, 2)) for q in range(4)]), [0], 1024)
    add(cells(1, [(step(y, 2), q) for q in range(4)]), [0], 1024)
    add(cells(2, [(a, b) for a in range(4) for b in range(4)]), both(step(z, 2)), 128)
    out_ref[...] = acc[...].astype(BF)
    for copy in sent:
        copy.wait_send()


def sems(*shape):
    return pltpu.SemaphoreType.DMA(shape)


ANY = pl.BlockSpec(memory_space=pl.ANY)
VMEM = pl.BlockSpec(memory_space=pltpu.VMEM)


def shards(
    occ_coef, vir_coef, atom_counts, occ_index, vir_index, interaction, window_charges, panel_start
):
    idx = jnp.broadcast_to(jnp.concatenate([occ_index, vir_index])[None], (8, 128))
    block = pl.pallas_call(
        front,
        out_shape=jax.ShapeDtypeStruct((3, 128, 128), BF),
        in_specs=[ANY, ANY, ANY, VMEM, ANY],
        out_specs=VMEM,
        scratch_shapes=[
            pltpu.VMEM((16, 8, 128), jnp.int32),
            pltpu.VMEM((16, 64, 128), BF),
            pltpu.VMEM((16, 128, 128), BF),
            pltpu.VMEM((1024, 1024), BF),
            pltpu.VMEM((1024, 2048), BF),
            pltpu.VMEM((2048, 768), BF),
            pltpu.VMEM((16, 64, 128), BF),
            pltpu.VMEM((16, 64, 128), BF),
            pltpu.VMEM((4, 4, 64, 768), BF),
            pltpu.VMEM((768, 384), BF),
            pltpu.VMEM((512, 384), F32),
            pltpu.VMEM((512, 384), F32),
            pltpu.VMEM((4, 128, 384), F32),
            pltpu.VMEM((4, 2, 128, 384), BF),
            sems(15), sems(16), sems(15), sems(16), sems(15), sems(16), sems(15), sems(16),
            sems(16), sems(16), sems(4), sems(4), sems(1),
        ],
        compiler_params=pltpu.CompilerParams(
            collective_id=0, has_side_effects=True, vmem_limit_bytes=56 * 2**20
        ),
    )(idx, occ_coef, vir_coef, atom_counts, interaction)
    coupling = pl.pallas_call(
        back,
        out_shape=jax.ShapeDtypeStruct((1024, 1024), BF),
        in_specs=[VMEM, ANY],
        out_specs=VMEM,
        scratch_shapes=[
            pltpu.VMEM((3, 4, 4, 1024, 128), BF),
            pltpu.VMEM((48, 1024, 128), BF),
            pltpu.VMEM((1024, 1024), F32),
            sems(3, 20), sems(3, 20), sems(3, 16), sems(3, 16), sems(1),
        ],
        compiler_params=pltpu.CompilerParams(
            collective_id=1, has_side_effects=True, vmem_limit_bytes=56 * 2**20
        ),
    )(block, window_charges)
    panel_index = lax.broadcasted_iota(jnp.int32, coupling.shape, 0)
    window_index = lax.axis_index(("row", "col")) * window_charges.shape[0] + lax.broadcasted_iota(
        jnp.int32, coupling.shape, 1
    )
    upper_mask = window_index >= panel_start[0] + panel_index
    return jnp.where(upper_mask, coupling, jnp.zeros_like(coupling))


def solution(mesh):
    placed = (
        P("row", "col"),
        P("row", "col"),
        P("col", None),
        P("row"),
        P("row"),
        P("col", "row"),
        P(("row", "col"), None),
        P(),
    )
    return jax.shard_map(
        shards, mesh=mesh, in_specs=placed, out_specs=P(None, ("row", "col")), check_vma=False
    )
```

```python
import jax
import jax.numpy as jnp
from jax import lax
from jax.experimental import pallas as pl
from jax.experimental.pallas import tpu as pltpu
from jax.sharding import PartitionSpec as P

MESH = pl.DeviceIdType.MESH
BF = jnp.bfloat16
F32 = jnp.float32


def place():
    row, col = lax.axis_index("row"), lax.axis_index("col")
    return lax.div(row, 4), lax.rem(row, 4), lax.div(col, 2), lax.rem(col, 2)


def step(c, d):
    return lax.rem(c + d, 4)


def device(y, x, z, k):
    return (y * 4 + x, z * 2 + k)


def send(src, dst, send_sem, recv_sem, target):
    copy = pltpu.make_async_remote_copy(
        src_ref=src, dst_ref=dst, send_sem=send_sem, recv_sem=recv_sem, device_id=target, device_id_type=MESH
    )
    copy.start()
    return copy


def arrived(ref, send_sem, recv_sem, me):
    pltpu.make_async_remote_copy(
        src_ref=ref, dst_ref=ref, send_sem=send_sem, recv_sem=recv_sem, device_id=me, device_id_type=MESH
    ).wait_recv()


def greet(targets):
    barrier = pltpu.get_barrier_semaphore()
    for target in targets:
        pl.semaphore_signal(barrier, inc=1, device_id=target, device_id_type=MESH)
    pl.semaphore_wait(barrier, len(targets))


def iota(shape, dim):
    return lax.broadcasted_iota(jnp.int32, shape, dim).astype(F32)


def panel_kernel(occ_index, vir_index, occ_hbm, vir_hbm, counts_ref, inter_hbm, win_hbm, out_ref,
                 idx_own, idx_all, occ_t, vir_t, pick_occ, pick_vir, member, dens_out, dens, charges_out, charges,
                 inter, half_out, half_in, pot, win, acc,
                 idx_s, idx_r, occ_s, occ_r, vir_s, vir_r, dens_s, dens_r, int_s, int_r, swap_s, swap_r,
                 ag_s, ag_r, half_s, half_r, ici_s, ici_r, d2d_s, d2d_r, loc):
    y, x, z, k = place()
    me = device(y, x, z, k)
    r = y * 4 + x
    twin = device(y, x, z, 1 - k)
    plane = [(step(y, d // 4), step(x, d % 4)) for d in range(1, 16)]
    idx_own[...] = jnp.broadcast_to(jnp.concatenate([occ_index[...], vir_index[...]], axis=1), (8, 128))
    greet(
        [device(yy, xx, z, k) for yy, xx in plane]
        + [device(y, x, step(z, d), k) for d in (1, 2, 3)]
        + [twin]
    )
    ups = {"y": device(step(y, 1), x, z, k), "x": device(y, step(x, 1), z, k), "z": device(y, x, step(z, 1), k)}
    downs = {"y": device(step(y, 3), x, z, k), "x": device(y, step(x, 3), z, k), "z": device(y, x, step(z, 3), k)}
    fars = {"y": device(step(y, 2), x, z, k), "x": device(y, step(x, 2), z, k), "z": device(y, x, step(z, 2), k)}
    at = {"y": y, "x": x, "z": z}
    sent = []
    own_cols = pl.ds(pl.multiple_of(r * 128, 128), 128)
    own_inter = pltpu.make_async_copy(inter_hbm, inter.at[z], loc.at[0])
    for copy in (
        pltpu.make_async_copy(idx_own, idx_all.at[r], idx_r.at[r]),
        pltpu.make_async_copy(occ_hbm.at[:, own_cols], occ_t.at[r], occ_r.at[r]),
        pltpu.make_async_copy(vir_hbm.at[:, own_cols], vir_t.at[r], vir_r.at[r]),
        own_inter,
    ):
        copy.start()
    for d, (yy, xx) in enumerate(plane):
        sent.append(send(idx_own, idx_all.at[r], idx_s.at[d], idx_r.at[r], device(yy, xx, z, k)))
    for d, (yy, xx) in enumerate(plane):
        cols = pl.ds(pl.multiple_of((yy * 4 + xx) * 128, 128), 128)
        sent.append(send(occ_hbm.at[:, cols], occ_t.at[r], occ_s.at[d], occ_r.at[r], device(yy, xx, z, k)))
    for d, (yy, xx) in enumerate(plane):
        cols = pl.ds(pl.multiple_of((yy * 4 + xx) * 128, 128), 128)
        sent.append(send(vir_hbm.at[:, cols], vir_t.at[r], vir_s.at[d], vir_r.at[r], device(yy, xx, z, k)))
    sent.append(send(inter_hbm, inter.at[z], int_s.at[0], int_r.at[0], ups["z"]))
    sent.append(send(inter_hbm, inter.at[z], int_s.at[1], int_r.at[1], downs["z"]))
    counts = counts_ref[...].astype(F32)
    upper = (iota((768, 768), 0) <= iota((768, 768), 1)).astype(BF)
    ends = jnp.dot(jnp.broadcast_to(counts, (8, 768)).astype(BF), upper, preferred_element_type=F32)[0:1]
    starts = ends - counts

    def members(i, carry):
        basis = iota((256, 768), 0) + (i * 256).astype(F32)
        inside = jnp.logical_and(basis >= starts, basis < ends)
        member[pl.ds(pl.multiple_of(i * 256, 256), 256), :] = jnp.where(inside, 1.0, 0.0).astype(BF)
        return carry

    lax.fori_loop(0, 8, members, 0)
    for s in range(16):
        arrived(idx_all.at[s], idx_s.at[0], idx_r.at[s], me)

    def picks(s, carry):
        line = idx_all[s][0:1].astype(F32)
        mine = iota((128, 128), 0) == iota((128, 128), 1)
        column = jnp.sum(jnp.where(mine, jnp.broadcast_to(line, (128, 128)), 0.0), axis=1, keepdims=True)
        rows = pl.ds(pl.multiple_of(s * 64, 64), 64)
        pick_occ[rows, :] = jnp.where(column[0:64] == iota((64, 1024), 1), 1.0, 0.0).astype(BF)
        pick_vir[rows, :] = jnp.where(column[64:128] == iota((64, 2048), 1), 1.0, 0.0).astype(BF)
        return carry

    lax.fori_loop(0, 16, picks, 0)
    for s in range(16):
        arrived(occ_t.at[s], occ_s.at[0], occ_r.at[s], me)
    for s in range(16):
        arrived(vir_t.at[s], vir_s.at[0], vir_r.at[s], me)
    occ_rows, vir_rows = occ_t[...].reshape(1024, 128), vir_t[...].reshape(2048, 128)
    n = 0
    for dy in (2, 1, 3, 0):
        yy = step(y, dy)
        rows = pl.ds(pl.multiple_of(yy * 256, 256), 256)
        first_rows = jnp.dot(pick_occ[rows, :], occ_rows, preferred_element_type=F32)
        second_rows = jnp.dot(pick_vir[rows, :], vir_rows, preferred_element_type=F32)
        dens_out[pl.ds(yy * 4, 4)] = (first_rows * second_rows).astype(BF).reshape(4, 64, 128)
        for dx in (2, 1, 3, 0):
            xx = step(x, dx)
            other = yy * 4 + xx
            if dy == 0 and dx == 0:
                pltpu.make_async_copy(dens_out.at[r], dens.at[r], dens_r.at[r]).start()
            else:
                sent.append(send(dens_out.at[other], dens.at[r], dens_s.at[n], dens_r.at[r], device(yy, xx, z, k)))
                n += 1

    def load(i, carry):
        cols = pl.ds(pl.multiple_of(i * 128, 128), 128)
        pltpu.make_async_copy(win_hbm.at[:, cols], win.at[i], loc.at[1]).start()
        return carry

    lax.fori_loop(0, 48, load, 0)
    for s in range(16):
        arrived(dens.at[s], dens_s.at[0], dens_r.at[s], me)
    density = jnp.concatenate([dens[s] for s in range(16)], axis=1)
    own_charges = jnp.dot(density, member[...], preferred_element_type=F32).astype(BF)
    charges_out[...] = own_charges.reshape(4, 16, 768)
    charges[y, x, z] = charges_out[z]
    for d in (1, 2, 3):
        zz = step(z, d)
        sent.append(send(charges_out.at[zz], charges.at[y, x, z], swap_s.at[d], swap_r.at[d], device(y, x, zz, k)))
    below, above = step(z, 3), step(z, 1)
    arrived(inter.at[below], int_s.at[0], int_r.at[0], me)
    top, bottom = pl.ds(0, 384), pl.ds(384, 384)
    sent.append(send(inter.at[below, top], inter.at[below, top], int_s.at[2], int_r.at[2], ups["z"]))
    arrived(inter.at[above], int_s.at[1], int_r.at[1], me)
    sent.append(send(inter.at[above, bottom], inter.at[above, bottom], int_s.at[3], int_r.at[3], downs["z"]))
    for d in (1, 2, 3):
        arrived(charges.at[y, x, step(z, 4 - d)], swap_s.at[d], swap_r.at[d], me)
    views = (
        lambda a, b, h=None: charges.at[b, a, pl.ds(0, 2)],
        lambda a, b, h=None: charges.at[a, b, pl.ds(2, 2)],
    )
    axes = (("x", "y"), ("y", "x"))

    def plane_sems(part, i):
        return ag_s.at[part, i], ag_r.at[part, i]

    def plane_block(part, a, b):
        return views[part](step(at[axes[part][0]], a), step(at[axes[part][1]], b))

    def plane_second(part, a):
        ref = plane_block(part, a, 0)
        sent.append(send(ref, ref, *plane_sems(part, 3 + a), ups[axes[part][1]]))
        sent.append(send(ref, ref, *plane_sems(part, 7 + a), downs[axes[part][1]]))

    def plane_first_arrival(part, a):
        arrived(plane_block(part, a, 0), *plane_sems(part, {3: 0, 1: 1, 2: 2}[a]), me)
        plane_second(part, a)

    def plane_second_arrival(part, a):
        ref = plane_block(part, a, 3)
        arrived(ref, *plane_sems(part, 3 + a), me)
        if a in (0, 2):
            sent.append(send(ref, ref, *plane_sems(part, 11 + a), ups[axes[part][1]]))
        ref = plane_block(part, a, 1)
        arrived(ref, *plane_sems(part, 7 + a), me)
        if a in (1, 3):
            sent.append(send(ref, ref, *plane_sems(part, 11 + a), downs[axes[part][1]]))

    for part in range(2):
        ref = plane_block(part, 0, 0)
        sent.append(send(ref, ref, *plane_sems(part, 0), ups[axes[part][0]]))
        sent.append(send(ref, ref, *plane_sems(part, 1), downs[axes[part][0]]))
        sent.append(send(ref, ref, *plane_sems(part, 2), fars[axes[part][0]]))
    for part in range(2):
        plane_second(part, 0)
    for what, a in ((1, 3), (1, 1), (2, 0), (1, 2), (2, 3), (2, 1), (2, 2)):
        for part in range(2):
            (plane_first_arrival if what == 1 else plane_second_arrival)(part, a)
    for a in range(4):
        for part in range(2):
            arrived(plane_block(part, a, 2), *plane_sems(part, 11 + a), me)
    own_inter.wait()
    arrived(inter.at[step(z, 2), top], int_s.at[2], int_r.at[2], me)
    arrived(inter.at[step(z, 2), bottom], int_s.at[3], int_r.at[3], me)

    def product(half):
        lhs = jnp.concatenate([charges[pl.ds(2 * half, 2), :, zz].reshape(128, 768) for zz in range(4)], axis=1)
        return jnp.dot(lhs, inter[...].reshape(3072, 384), preferred_element_type=F32)

    half_out[...] = product(1 - k)
    swap = send(half_out, half_in, half_s.at[0], half_r.at[0], twin)
    sent.append(swap)
    total = product(k)
    swap.wait_recv()
    total = (total + half_in[...]).astype(BF)

    def rows(s, kk=k, n=128):
        return pl.ds(pl.multiple_of(kk * 512 + s * 128, 128), n)

    def half_rows(kk=k):
        return pl.ds(pl.multiple_of(kk * 512, 512), 512)

    for j in range(3):
        pot[j, y, x, rows(z), :] = total[:, 128 * j:128 * j + 128]
    orders = ("zyx", "xzy", "yxz")
    first = (
        lambda s: pot.at[0, y, x, rows(s)],
        lambda s: pot.at[1, y, s, rows(z)],
        lambda s: pot.at[2, s, x, rows(z)],
    )

    def two(h):
        return slice(None) if h is None else pl.ds(2 * h, 2)

    second = (
        lambda s, h=None, kk=k: pot.at[0, s, x, half_rows(kk) if h is None else pl.ds(pl.multiple_of(kk * 512 + 256 * h, 256), 256)],
        lambda s, h=None, kk=k: pot.at[1, y, two(h), rows(s, kk)],
        lambda s, h=None, kk=k: pot.at[2, two(h), s, rows(z, kk)],
    )
    third = (
        lambda s, q, kk=k: pot.at[0, q, s, half_rows(kk)],
        lambda s, q, kk=k: pot.at[1, s, :, rows(q, kk)],
        lambda s, q, kk=k: pot.at[2, :, q, rows(s, kk)],
    )
    n_d2d = [0, 0, 0]

    def ici(j, i):
        return ici_s.at[j, i], ici_r.at[j, i]

    def share(j, ref):
        n_d2d[j] += 1
        pair = d2d_s.at[j, n_d2d[j] - 1], d2d_r.at[j, n_d2d[j] - 1]
        sent.append(send(ref, ref, *pair, twin))
        return pair

    c1, c2, c3 = ([at[orders[j][level]] for j in range(3)] for level in range(3))
    shared, chunks = {}, {}

    def third_send(j, a):
        ref = third[j](c3[j], step(c2[j], a))
        sent.append(send(ref, ref, *ici(j, 7 + a), ups[orders[j][2]]))
        sent.append(send(ref, ref, *ici(j, 11 + a), downs[orders[j][2]]))

    def third_arrival(a):
        for j in range(3):
            q = step(c2[j], a)
            ref = third[j](step(c3[j], 3), q)
            arrived(ref, *ici(j, 7 + a), me)
            if a in (0, 2):
                sent.append(send(ref, ref, *ici(j, 15 + a), ups[orders[j][2]]))
            chunks[j, a, 3] = share(j, ref)
            ref = third[j](step(c3[j], 1), q)
            arrived(ref, *ici(j, 11 + a), me)
            if a in (1, 3):
                sent.append(send(ref, ref, *ici(j, 15 + a), downs[orders[j][2]]))
            chunks[j, a, 1] = share(j, ref)

    def far_arrival(a):
        for j in range(3):
            ref = third[j](step(c3[j], 2), step(c2[j], a))
            arrived(ref, *ici(j, 15 + a), me)
            chunks[j, a, 2] = share(j, ref)

    def second_twin(j):
        for a in range(4):
            arrived(second[j](step(c2[j], a), kk=1 - k), *shared[j, a], me)

    def chunk_twin(j, a, b):
        arrived(third[j](step(c3[j], b), step(c2[j], a), 1 - k), *chunks[j, a, b], me)

    for j in range(3):
        ref = first[j](c1[j])
        sent.append(send(ref, ref, *ici(j, 0), ups[orders[j][0]]))
        sent.append(send(ref, ref, *ici(j, 1), downs[orders[j][0]]))
        sent.append(send(ref, ref, *ici(j, 2), fars[orders[j][0]]))
    pltpu.make_async_copy(win, win, loc.at[1]).wait()
    for j in range(3):
        for i, d in enumerate((3, 1, 2)):
            arrived(first[j](step(c1[j], d)), *ici(j, i), me)
        ref = second[j](c2[j])
        sent.append(send(ref, ref, *ici(j, 3), ups[orders[j][1]]))
        sent.append(send(ref, ref, *ici(j, 4), downs[orders[j][1]]))
        third_send(j, 0)
        shared[j, 0] = share(j, ref)
    for j in range(3):
        ref = second[j](step(c2[j], 3))
        arrived(ref, *ici(j, 3), me)
        half = second[j](step(c2[j], 3), 0)
        sent.append(send(half, half, *ici(j, 5), ups[orders[j][1]]))
        third_send(j, 3)
        shared[j, 3] = share(j, ref)
        ref = second[j](step(c2[j], 1))
        arrived(ref, *ici(j, 4), me)
        half = second[j](step(c2[j], 1), 1)
        sent.append(send(half, half, *ici(j, 6), downs[orders[j][1]]))
        third_send(j, 1)
        shared[j, 1] = share(j, ref)
    third_arrival(0)
    for j in range(3):
        far = step(c2[j], 2)
        arrived(second[j](far, 0), *ici(j, 5), me)
        arrived(second[j](far, 1), *ici(j, 6), me)
        third_send(j, 2)
        shared[j, 2] = share(j, second[j](far))

    started = [False]

    def add(points, row_starts, size):
        lhs = jnp.concatenate([
            jnp.concatenate([pot[j, yy, xx, pl.ds(pl.multiple_of(s, 128), size), :] for s in row_starts], axis=0)
            for j, yy, xx in points], axis=1)
        rhs = jnp.concatenate([win[(yy * 4 + xx) * 3 + j] for j, yy, xx in points], axis=1)
        value = lax.dot_general(lhs, rhs, (((1,), (1,)), ((), ())), preferred_element_type=F32)
        if not started[0]:
            acc[...] = value
            started[0] = True
            return
        for i, s in enumerate(row_starts):
            where = pl.ds(pl.multiple_of(s, 128), size)
            acc[where, :] += value[i * size:(i + 1) * size]

    def both(s):
        return [s * 128, 512 + s * 128]

    def add_second(j):
        second_twin(j)
        if j == 0:
            add([(0, q, x) for q in range(4)], [0], 1024)
        if j == 1:
            add([(1, y, q) for q in range(4)], [0], 1024)
        if j == 2:
            add([(2, a, b) for a in range(4) for b in range(4)], both(z), 128)

    def add_third(j, chunk_pair, others):
        for a in chunk_pair:
            for b in others:
                chunk_twin(j, a, b)
        qs = [step(c2[j], a) for a in chunk_pair]
        ss = [step(c3[j], b) for b in others]
        if j == 0:
            add([(0, q, s) for q in qs for s in ss], [0], 1024)
        if j == 1:
            add([(1, s, b) for s in ss for b in range(4)], both(qs[0]) + both(qs[1]), 128)
        if j == 2:
            add([(2, a, q) for a in range(4) for q in qs], [v for s in ss for v in both(s)], 128)

    add_second(0)
    third_arrival(3)
    add_second(1)
    add_second(2)
    third_arrival(1)
    add_third(0, (0, 3), (3, 1))
    add_third(1, (0, 3), (3, 1))
    third_arrival(2)
    add_third(2, (0, 3), (3, 1))
    far_arrival(0)
    far_arrival(3)
    for j in range(3):
        add_third(j, (1, 2), (3, 1))
    far_arrival(1)
    far_arrival(2)
    for j in range(3):
        add_third(j, (0, 3), (2,))
    for j in range(3):
        add_third(j, (1, 2), (2,))
    for kk in range(2):
        for zz in range(4):
            for i in range(8):
                out_ref[(kk * 8 + i) * 64 + zz * 16:(kk * 8 + i) * 64 + zz * 16 + 16] = acc[
                    kk * 512 + zz * 128 + i * 16:kk * 512 + zz * 128 + i * 16 + 16].astype(BF)
    for copy in sent:
        copy.wait_send()


def sems(*shape):
    return pltpu.SemaphoreType.DMA(shape)


ANY = pl.BlockSpec(memory_space=pl.ANY)
VMEM = pl.BlockSpec(memory_space=pltpu.VMEM)


def shards(
    occ_coef, vir_coef, atom_counts, occ_index, vir_index, interaction, window_charges, panel_start
):
    coupling = pl.pallas_call(
        panel_kernel,
        out_shape=jax.ShapeDtypeStruct((1024, 1024), BF),
        in_specs=[VMEM, VMEM, ANY, ANY, VMEM, ANY, ANY],
        out_specs=VMEM,
        scratch_shapes=[
            pltpu.VMEM((8, 128), jnp.int32),
            pltpu.VMEM((16, 8, 128), jnp.int32),
            pltpu.VMEM((16, 64, 128), BF),
            pltpu.VMEM((16, 128, 128), BF),
            pltpu.VMEM((1024, 1024), BF),
            pltpu.VMEM((1024, 2048), BF),
            pltpu.VMEM((2048, 768), BF),
            pltpu.VMEM((16, 64, 128), BF),
            pltpu.VMEM((16, 64, 128), BF),
            pltpu.VMEM((4, 16, 768), BF),
            pltpu.VMEM((4, 4, 4, 16, 768), BF),
            pltpu.VMEM((4, 768, 384), BF),
            pltpu.VMEM((128, 384), F32),
            pltpu.VMEM((128, 384), F32),
            pltpu.VMEM((3, 4, 4, 1024, 128), BF),
            pltpu.VMEM((48, 1024, 128), BF),
            pltpu.VMEM((1024, 1024), F32),
            sems(15), sems(16), sems(15), sems(16), sems(15), sems(16), sems(15), sems(16),
            sems(4), sems(4), sems(4), sems(4), sems(2, 15), sems(2, 15), sems(1), sems(1),
            sems(3, 19), sems(3, 19), sems(3, 16), sems(3, 16), sems(2),
        ],
        compiler_params=pltpu.CompilerParams(
            collective_id=0, has_side_effects=True, vmem_limit_bytes=60 * 2**20
        ),
    )(occ_index[None], vir_index[None], occ_coef, vir_coef, atom_counts, interaction, window_charges)
    panel_index = lax.broadcasted_iota(jnp.int32, coupling.shape, 0)
    window_index = lax.axis_index(("row", "col")) * window_charges.shape[0] + lax.broadcasted_iota(
        jnp.int32, coupling.shape, 1
    )
    upper_mask = window_index >= panel_start[0] + panel_index
    return jnp.where(upper_mask, coupling, jnp.zeros_like(coupling))


def solution(mesh):
    placed = (
        P("row", "col"),
        P("row", "col"),
        P("col", None),
        P("row"),
        P("row"),
        P("col", "row"),
        P(("row", "col"), None),
        P(),
    )
    return jax.shard_map(
        shards, mesh=mesh, in_specs=placed, out_specs=P(None, ("row", "col")), check_vma=False
    )
```

```python
import jax
import jax.numpy as jnp
from jax import lax
from jax.experimental import pallas as pl
from jax.experimental.pallas import tpu as pltpu
from jax.sharding import PartitionSpec as P

MESH = pl.DeviceIdType.MESH
BF = jnp.bfloat16
F32 = jnp.float32


def place():
    row, col = lax.axis_index("row"), lax.axis_index("col")
    return lax.div(row, 4), lax.rem(row, 4), lax.div(col, 2), lax.rem(col, 2)


def step(c, d):
    return lax.rem(c + d, 4)


def device(y, x, z, k):
    return (y * 4 + x, z * 2 + k)


def send(src, dst, send_sem, recv_sem, target):
    copy = pltpu.make_async_remote_copy(
        src_ref=src, dst_ref=dst, send_sem=send_sem, recv_sem=recv_sem, device_id=target, device_id_type=MESH
    )
    copy.start()


def left(ref, send_sem, me):
    pltpu.make_async_remote_copy(
        src_ref=ref, dst_ref=ref, send_sem=send_sem, recv_sem=send_sem, device_id=me, device_id_type=MESH
    ).wait_send()


def arrived(ref, send_sem, recv_sem, me):
    pltpu.make_async_remote_copy(
        src_ref=ref, dst_ref=ref, send_sem=send_sem, recv_sem=recv_sem, device_id=me, device_id_type=MESH
    ).wait_recv()


def iota(shape, dim):
    return lax.broadcasted_iota(jnp.int32, shape, dim).astype(F32)


def panel_kernel(occ_index, vir_index, occ_hbm, vir_hbm, counts_hbm, inter_hbm, win_hbm, out_ref,
                 occ_own, vir_own, counts_ref, idx_own, idx_all, occ_t, vir_t, pick_occ, pick_vir, picked_occ, picked_vir, member, dens_out, dens, charges_out, charges,
                 inter, halves, half_in, pot, win, acc,
                 idx_s, idx_r, occ_s, occ_r, vir_s, vir_r, dens_s, dens_r, int_s, int_r, swap_s, swap_r,
                 ag_s, ag_r, half_s, half_r, ici_s, ici_r, d2d_s, d2d_r, loc):
    y, x, z, k = place()
    me = device(y, x, z, k)
    r = y * 4 + x
    twin = device(y, x, z, 1 - k)
    plane = [(step(y, dy), step(x, dx)) for dy in (0, 1, 3, 2) for dx in range(4) if dy or dx]
    small = [
        pltpu.make_async_copy(occ_index, occ_own, loc.at[2]),
        pltpu.make_async_copy(vir_index, vir_own, loc.at[3]),
        pltpu.make_async_copy(counts_hbm, counts_ref, loc.at[4]),
    ]
    for copy in small:
        copy.start()
    partners = (
        [device(yy, xx, z, k) for yy, xx in plane]
        + [device(y, x, step(z, d), k) for d in (1, 2, 3)]
        + [twin]
    )
    barrier = pltpu.get_barrier_semaphore()
    for target in partners:
        pl.semaphore_signal(barrier, inc=1, device_id=target, device_id_type=MESH)
    for copy in small:
        copy.wait()
    idx_own[...] = jnp.broadcast_to(jnp.concatenate([occ_own[...], vir_own[...]], axis=1), (8, 128))
    pl.semaphore_wait(barrier, len(partners))
    ups = {"y": device(step(y, 1), x, z, k), "x": device(y, step(x, 1), z, k), "z": device(y, x, step(z, 1), k)}
    downs = {"y": device(step(y, 3), x, z, k), "x": device(y, step(x, 3), z, k), "z": device(y, x, step(z, 3), k)}
    fars = {"y": device(step(y, 2), x, z, k), "x": device(y, step(x, 2), z, k), "z": device(y, x, step(z, 2), k)}
    at = {"y": y, "x": x, "z": z}
    own_cols = pl.ds(pl.multiple_of(r * 128, 128), 128)
    own_inter = pltpu.make_async_copy(inter_hbm, inter.at[z], loc.at[0])
    for copy in (
        pltpu.make_async_copy(idx_own, idx_all.at[r], idx_r.at[0]),
        pltpu.make_async_copy(occ_hbm.at[:, own_cols], occ_t.at[r], occ_r.at[0]),
        pltpu.make_async_copy(vir_hbm.at[:, own_cols], vir_t.at[r], vir_r.at[y]),
        own_inter,
    ):
        copy.start()
    for d, (yy, xx) in enumerate(plane):
        send(idx_own, idx_all.at[r], idx_s.at[0], idx_r.at[0], device(yy, xx, z, k))
    for d, (yy, xx) in enumerate(plane):
        cols = pl.ds(pl.multiple_of((yy * 4 + xx) * 128, 128), 128)
        send(occ_hbm.at[:, cols], occ_t.at[r], occ_s.at[0], occ_r.at[0], device(yy, xx, z, k))
    for d, (yy, xx) in enumerate(plane):
        cols = pl.ds(pl.multiple_of((yy * 4 + xx) * 128, 128), 128)
        send(vir_hbm.at[:, cols], vir_t.at[r], vir_s.at[0], vir_r.at[y], device(yy, xx, z, k))
    send(inter_hbm, inter.at[z], int_s.at[0], int_r.at[0], ups["z"])
    send(inter_hbm, inter.at[z], int_s.at[0], int_r.at[1], downs["z"])
    def load(i, carry):
        cols = pl.ds(pl.multiple_of(i * 128, 128), 128)
        pltpu.make_async_copy(win_hbm.at[:, cols], win.at[i], loc.at[1]).start()
        return carry

    lax.fori_loop(0, 48, load, 0)
    counts = counts_ref[...].astype(F32)
    upper = (iota((768, 768), 0) <= iota((768, 768), 1)).astype(BF)
    ends = jnp.dot(jnp.broadcast_to(counts, (8, 768)).astype(BF), upper, preferred_element_type=F32)[0:1]
    starts = ends - counts

    def members(i, carry):
        basis = iota((256, 768), 0) + (i * 256).astype(F32)
        inside = jnp.logical_and(basis >= starts, basis < ends)
        member[pl.ds(pl.multiple_of(i * 256, 256), 256), :] = jnp.where(inside, 1.0, 0.0).astype(BF)
        return carry

    lax.fori_loop(0, 8, members, 0)
    arrived(idx_all, idx_s.at[0], idx_r.at[0], me)

    def picks(s, carry):
        line = idx_all[s][0:1].astype(F32)
        mine = iota((128, 128), 0) == iota((128, 128), 1)
        column = jnp.sum(jnp.where(mine, jnp.broadcast_to(line, (128, 128)), 0.0), axis=1, keepdims=True)
        rows = pl.ds(pl.multiple_of(s * 64, 64), 64)
        pick_occ[rows, :] = jnp.where(column[0:64] == iota((64, 1024), 1), 1.0, 0.0).astype(BF)
        pick_vir[rows, :] = jnp.where(column[64:128] == iota((64, 2048), 1), 1.0, 0.0).astype(BF)
        return carry

    lax.fori_loop(0, 16, picks, 0)
    arrived(occ_t, occ_s.at[0], occ_r.at[0], me)
    picked_occ[...] = jnp.dot(pick_occ[...], occ_t[...].reshape(1024, 128), preferred_element_type=F32)

    def vir_line(rows, yy):
        cols = pl.ds(pl.multiple_of(yy * 512, 512), 512)
        return jnp.dot(
            pick_vir[rows, cols], vir_t[pl.ds(yy * 4, 4)].reshape(512, 128), preferred_element_type=F32
        )

    for i, dy in enumerate((0, 3, 1, 2)):
        yy = step(y, dy)
        arrived(vir_t.at[pl.ds(yy * 4, 4)], vir_s.at[0], vir_r.at[yy], me)
        if i == 0:
            picked_vir[...] = vir_line(slice(None), yy)
        elif i < 3:
            picked_vir[...] += vir_line(slice(None), yy)
    for dy in (2, 1, 3, 0):
        yy = step(y, dy)
        rows = pl.ds(pl.multiple_of(yy * 256, 256), 256)
        second_rows = picked_vir[rows, :] + vir_line(rows, step(y, 2))
        dens_out[pl.ds(yy * 4, 4)] = (picked_occ[rows, :] * second_rows).astype(BF).reshape(4, 64, 128)
        for dx in (2, 1, 3, 0):
            xx = step(x, dx)
            other = yy * 4 + xx
            if dy == 0 and dx == 0:
                pltpu.make_async_copy(dens_out.at[r], dens.at[r], dens_r.at[0]).start()
            else:
                send(dens_out.at[other], dens.at[r], dens_s.at[0], dens_r.at[0], device(yy, xx, z, k))

    left(idx_all.at[pl.ds(0, 15)], idx_s.at[0], me)
    left(occ_t.at[pl.ds(0, 15)], occ_s.at[0], me)
    left(vir_t.at[pl.ds(0, 15)], vir_s.at[0], me)
    arrived(dens, dens_s.at[0], dens_r.at[0], me)
    density = jnp.concatenate([dens[s] for s in range(16)], axis=1)
    own_charges = jnp.dot(density, member[...], preferred_element_type=F32).astype(BF)
    charges_out[...] = own_charges.reshape(4, 16, 768)
    charges[y, x, z] = charges_out[z]
    for d in (1, 2, 3):
        zz = step(z, d)
        send(charges_out.at[zz], charges.at[y, x, z], swap_s.at[0], swap_r.at[0], device(y, x, zz, k))
    below, above = step(z, 3), step(z, 1)
    arrived(inter.at[below], int_s.at[0], int_r.at[0], me)
    top, bottom = pl.ds(0, 384), pl.ds(384, 384)
    send(inter.at[below, top], inter.at[below, top], int_s.at[0], int_r.at[2], ups["z"])
    arrived(inter.at[above], int_s.at[0], int_r.at[1], me)
    send(inter.at[above, bottom], inter.at[above, bottom], int_s.at[0], int_r.at[3], downs["z"])
    left(dens.at[pl.ds(0, 15)], dens_s.at[0], me)
    arrived(charges_out.at[pl.ds(0, 3)], swap_s.at[0], swap_r.at[0], me)
    views = (
        lambda a, b, h=None: charges.at[b, a, pl.ds(0, 2)],
        lambda a, b, h=None: charges.at[a, b, pl.ds(2, 2)],
    )
    axes = (("x", "y"), ("y", "x"))

    def plane_sems(part, i):
        return ag_s.at[0], ag_r.at[part, i]

    def plane_block(part, a, b):
        return views[part](step(at[axes[part][0]], a), step(at[axes[part][1]], b))

    def plane_second(part, a):
        ref = plane_block(part, a, 0)
        send(ref, ref, *plane_sems(part, 3 + a), ups[axes[part][1]])
        send(ref, ref, *plane_sems(part, 7 + a), downs[axes[part][1]])

    def plane_first_arrival(part, a):
        arrived(plane_block(part, a, 0), *plane_sems(part, {3: 0, 1: 1, 2: 2}[a]), me)
        plane_second(part, a)

    def plane_second_arrival(part, a):
        ref = plane_block(part, a, 3)
        arrived(ref, *plane_sems(part, 3 + a), me)
        if a in (0, 2):
            send(ref, ref, *plane_sems(part, 11), ups[axes[part][1]])
        ref = plane_block(part, a, 1)
        arrived(ref, *plane_sems(part, 7 + a), me)
        if a in (1, 3):
            send(ref, ref, *plane_sems(part, 11), downs[axes[part][1]])

    for part in range(2):
        ref = plane_block(part, 0, 0)
        send(ref, ref, *plane_sems(part, 0), ups[axes[part][0]])
        send(ref, ref, *plane_sems(part, 1), downs[axes[part][0]])
        send(ref, ref, *plane_sems(part, 2), fars[axes[part][0]])
    for part in range(2):
        plane_second(part, 0)
    for what, a in ((1, 3), (1, 1), (2, 0), (1, 2), (2, 3), (2, 1), (2, 2)):
        for part in range(2):
            (plane_first_arrival if what == 1 else plane_second_arrival)(part, a)
    left(charges_out.at[pl.ds(0, 3)], swap_s.at[0], me)
    arrived(charges.at[step(y, 2), :, pl.ds(0, 2)], *plane_sems(0, 11), me)
    arrived(charges.at[:, step(x, 2), pl.ds(2, 2)], *plane_sems(1, 11), me)
    own_inter.wait()
    arrived(inter.at[step(z, 2), top], int_s.at[0], int_r.at[2], me)
    arrived(inter.at[step(z, 2), bottom], int_s.at[0], int_r.at[3], me)

    lhs = jnp.concatenate([charges[:, :, zz].reshape(256, 768) for zz in range(4)], axis=1)
    halves[...] = jnp.dot(lhs, inter[...].reshape(3072, 384), preferred_element_type=F32).reshape(2, 128, 384)
    send(halves.at[1 - k], half_in, half_s.at[0], half_r.at[0], twin)
    left(inter.at[pl.ds(0, 3)], int_s.at[0], me)
    left(pot.at[0, pl.ds(0, 3), pl.ds(0, 3), pl.ds(0, 640)], ag_s.at[0], me)
    arrived(half_in, half_s.at[0], half_r.at[0], me)
    total = (halves[k] + half_in[...]).astype(BF)

    def rows(s, kk=k, n=128):
        return pl.ds(pl.multiple_of(kk * 512 + s * 128, 128), n)

    def half_rows(kk=k):
        return pl.ds(pl.multiple_of(kk * 512, 512), 512)

    for j in range(3):
        pot[j, y, x, rows(z), :] = total[:, 128 * j:128 * j + 128]
    orders = ("zyx", "xzy", "yxz")
    first = (
        lambda s: pot.at[0, y, x, rows(s)],
        lambda s: pot.at[1, y, s, rows(z)],
        lambda s: pot.at[2, s, x, rows(z)],
    )

    def two(h):
        return slice(None) if h is None else pl.ds(2 * h, 2)

    second = (
        lambda s, h=None, kk=k: pot.at[0, s, x, half_rows(kk) if h is None else pl.ds(pl.multiple_of(kk * 512 + 256 * h, 256), 256)],
        lambda s, h=None, kk=k: pot.at[1, y, two(h), rows(s, kk)],
        lambda s, h=None, kk=k: pot.at[2, two(h), s, rows(z, kk)],
    )
    third = (
        lambda s, q, kk=k: pot.at[0, q, s, half_rows(kk)],
        lambda s, q, kk=k: pot.at[1, s, :, rows(q, kk)],
        lambda s, q, kk=k: pot.at[2, :, q, rows(s, kk)],
    )

    def ici(j, i):
        return ici_s.at[0], ici_r.at[j, i]

    def share(j, ref, group):
        send(ref, ref, d2d_s.at[0], d2d_r.at[j, group], twin)

    def shared(j, group, ref):
        arrived(ref, d2d_s.at[0], d2d_r.at[j, group], me)

    def chunk_group(a, b):
        return 1 + (a in (1, 2)) + 2 * (b == 2)

    c1, c2, c3 = ([at[orders[j][level]] for j in range(3)] for level in range(3))

    def third_send(j, a):
        ref = third[j](c3[j], step(c2[j], a))
        send(ref, ref, *ici(j, 7 + a), ups[orders[j][2]])
        send(ref, ref, *ici(j, 11 + a), downs[orders[j][2]])

    def third_arrival(a):
        for j in range(3):
            q = step(c2[j], a)
            ref = third[j](step(c3[j], 3), q)
            arrived(ref, *ici(j, 7 + a), me)
            if a in (0, 2):
                send(ref, ref, *ici(j, 15 + a), ups[orders[j][2]])
            share(j, ref, chunk_group(a, 3))
            ref = third[j](step(c3[j], 1), q)
            arrived(ref, *ici(j, 11 + a), me)
            if a in (1, 3):
                send(ref, ref, *ici(j, 15 + a), downs[orders[j][2]])
            share(j, ref, chunk_group(a, 1))

    def far_arrival(a):
        for j in range(3):
            ref = third[j](step(c3[j], 2), step(c2[j], a))
            arrived(ref, *ici(j, 15 + a), me)
            share(j, ref, chunk_group(a, 2))

    for j in range(3):
        ref = first[j](c1[j])
        send(ref, ref, *ici(j, 0), ups[orders[j][0]])
        send(ref, ref, *ici(j, 0), downs[orders[j][0]])
        send(ref, ref, *ici(j, 0), fars[orders[j][0]])
    pltpu.make_async_copy(win, win, loc.at[1]).wait()
    for j in range(3):
        arrived(pot.at[j, pl.ds(0, 3), 0, pl.ds(0, 128)], *ici(j, 0), me)
        ref = second[j](c2[j])
        send(ref, ref, *ici(j, 3), ups[orders[j][1]])
        send(ref, ref, *ici(j, 4), downs[orders[j][1]])
        third_send(j, 0)
        share(j, ref, 0)
    for j in range(3):
        ref = second[j](step(c2[j], 3))
        arrived(ref, *ici(j, 3), me)
        half = second[j](step(c2[j], 3), 0)
        send(half, half, *ici(j, 5), ups[orders[j][1]])
        third_send(j, 3)
        share(j, ref, 0)
        ref = second[j](step(c2[j], 1))
        arrived(ref, *ici(j, 4), me)
        half = second[j](step(c2[j], 1), 1)
        send(half, half, *ici(j, 6), downs[orders[j][1]])
        third_send(j, 1)
        share(j, ref, 0)
    third_arrival(0)
    for j in range(3):
        far = step(c2[j], 2)
        arrived(second[j](far, 0), *ici(j, 5), me)
        arrived(second[j](far, 1), *ici(j, 6), me)
        third_send(j, 2)
        share(j, second[j](far), 0)

    started = [False]

    def add(points, row_starts, size, last=False):
        lhs = jnp.concatenate([
            jnp.concatenate([pot[j, yy, xx, pl.ds(pl.multiple_of(s, 128), size), :] for s in row_starts], axis=0)
            for j, yy, xx in points], axis=1)
        rhs = jnp.concatenate([win[(yy * 4 + xx) * 3 + j] for j, yy, xx in points], axis=1)
        value = lax.dot_general(lhs, rhs, (((1,), (1,)), ((), ())), preferred_element_type=F32)
        if not started[0]:
            acc[...] = value
            started[0] = True
            return
        if last:
            value = (value + acc[...]).astype(BF)
            for kk in range(2):
                for zz in range(4):
                    for i in range(8):
                        here, there = kk * 512 + zz * 128 + i * 16, (kk * 8 + i) * 64 + zz * 16
                        out_ref[there:there + 16] = value[here:here + 16]
            return
        for i, s in enumerate(row_starts):
            where = pl.ds(pl.multiple_of(s, 128), size)
            acc[where, :] += value[i * size:(i + 1) * size]

    def both(s):
        return [s * 128, 512 + s * 128]

    def add_second(j):
        shared(j, 0, pot.at[j, :, 0, pl.ds(0, 512)])
        if j == 0:
            add([(0, q, x) for q in range(4)], [0], 1024)
        if j == 1:
            add([(1, y, q) for q in range(4)], [0], 1024)
        if j == 2:
            add([(2, a, b) for a in range(4) for b in range(4)], both(z), 128)

    def add_third(j, chunk_pair, others, last=False):
        shared(j, chunk_group(chunk_pair[0], others[0]), pot.at[j, pl.ds(0, 2 * len(others)), 0, pl.ds(0, 512)])
        qs = [step(c2[j], a) for a in chunk_pair]
        ss = [step(c3[j], b) for b in others]
        if j == 0:
            add([(0, q, s) for q in qs for s in ss], [0], 1024, last)
        if j == 1:
            add([(1, s, b) for s in ss for b in range(4)], both(qs[0]) + both(qs[1]), 128)
        if j == 2:
            add([(2, a, q) for a in range(4) for q in qs], [v for s in ss for v in both(s)], 128)

    third_arrival(3)
    add_second(0)
    add_second(1)
    third_arrival(1)
    add_second(2)
    add_third(0, (0, 3), (3, 1))
    third_arrival(2)
    add_third(1, (0, 3), (3, 1))
    add_third(2, (0, 3), (3, 1))
    far_arrival(0)
    for j in range(3):
        add_third(j, (1, 2), (3, 1))
    far_arrival(3)
    far_arrival(1)
    far_arrival(2)
    for j in range(3):
        add_third(j, (0, 3), (2,))
    for j in (1, 2, 0):
        add_third(j, (1, 2), (2,), j == 0)
    left(halves.at[1 - k], half_s.at[0], me)
    left(pot.at[:, :, :, half_rows()], d2d_s.at[0], me)
    left(pot.at[:, pl.ds(0, 3), pl.ds(0, 3), pl.ds(0, 896)], ici_s.at[0], me)


def mask_kernel(least, coupling, out_ref):
    shape = out_ref.shape
    ahead = lax.broadcasted_iota(jnp.int32, shape, 1) - lax.broadcasted_iota(jnp.int32, shape, 0)
    value = coupling[...].astype(F32)
    keep = ahead >= least[0] + pl.program_id(0) * shape[0]
    out_ref[...] = jnp.where(keep, value, jnp.zeros_like(value)).astype(BF)


def sems(*shape):
    return pltpu.SemaphoreType.DMA(shape)


ANY = pl.BlockSpec(memory_space=pl.ANY)
VMEM = pl.BlockSpec(memory_space=pltpu.VMEM)


def shards(
    occ_coef, vir_coef, atom_counts, occ_index, vir_index, interaction, window_charges, panel_start
):
    coupling = pl.pallas_call(
        panel_kernel,
        out_shape=jax.ShapeDtypeStruct((1024, 1024), BF),
        in_specs=[ANY] * 7,
        out_specs=VMEM,
        scratch_shapes=[
            pltpu.VMEM((1, 64), jnp.int32),
            pltpu.VMEM((1, 64), jnp.int32),
            pltpu.VMEM((1, 768), jnp.int32),
            pltpu.VMEM((8, 128), jnp.int32),
            pltpu.VMEM((16, 8, 128), jnp.int32),
            pltpu.VMEM((16, 64, 128), BF),
            pltpu.VMEM((16, 128, 128), BF),
            pltpu.VMEM((1024, 1024), BF),
            pltpu.VMEM((1024, 2048), BF),
            pltpu.VMEM((1024, 128), F32),
            pltpu.VMEM((1024, 128), F32),
            pltpu.VMEM((2048, 768), BF),
            pltpu.VMEM((16, 64, 128), BF),
            pltpu.VMEM((16, 64, 128), BF),
            pltpu.VMEM((4, 16, 768), BF),
            pltpu.VMEM((4, 4, 4, 16, 768), BF),
            pltpu.VMEM((4, 768, 384), BF),
            pltpu.VMEM((2, 128, 384), F32),
            pltpu.VMEM((128, 384), F32),
            pltpu.VMEM((3, 4, 4, 1024, 128), BF),
            pltpu.VMEM((48, 1024, 128), BF),
            pltpu.VMEM((1024, 1024), F32),
            sems(1), sems(1), sems(1), sems(1), sems(1), sems(4), sems(1), sems(1),
            sems(1), sems(4), sems(1), sems(1), sems(1), sems(2, 12), sems(1), sems(1),
            sems(1), sems(3, 19), sems(1), sems(3, 5), sems(5),
        ],
        compiler_params=pltpu.CompilerParams(
            collective_id=0, has_side_effects=True, vmem_limit_bytes=60 * 2**20
        ),
    )(occ_index[None], vir_index[None], occ_coef, vir_coef, atom_counts, interaction, window_charges)
    least = panel_start - lax.axis_index(("row", "col")) * window_charges.shape[0]
    return pl.pallas_call(
        mask_kernel,
        grid=(2,),
        out_shape=jax.ShapeDtypeStruct((1024, 1024), BF),
        in_specs=[pl.BlockSpec(memory_space=pltpu.SMEM), pl.BlockSpec((512, 1024), lambda i: (i, 0))],
        out_specs=pl.BlockSpec((512, 1024), lambda i: (i, 0)),
    )(least, coupling)


def solution(mesh):
    placed = (
        P("row", "col"),
        P("row", "col"),
        P("col", None),
        P("row"),
        P("row"),
        P("col", "row"),
        P(("row", "col"), None),
        P(),
    )
    return jax.shard_map(
        shards, mesh=mesh, in_specs=placed, out_specs=P(None, ("row", "col")), check_vma=False
    )
```

```python
import jax
import jax.numpy as jnp
from jax import lax
from jax.experimental import pallas as pl
from jax.experimental.pallas import tpu as pltpu
from jax.sharding import PartitionSpec as P

MESH = pl.DeviceIdType.MESH
BF = jnp.bfloat16
F32 = jnp.float32


def place():
    row, col = lax.axis_index("row"), lax.axis_index("col")
    return lax.div(row, 4), lax.rem(row, 4), lax.div(col, 2), lax.rem(col, 2)


def step(c, d):
    return lax.rem(c + d, 4)


def device(y, x, z, k):
    return (y * 4 + x, z * 2 + k)


def send(src, dst, send_sem, recv_sem, target):
    copy = pltpu.make_async_remote_copy(
        src_ref=src, dst_ref=dst, send_sem=send_sem, recv_sem=recv_sem, device_id=target, device_id_type=MESH
    )
    copy.start()


def left(ref, send_sem, me):
    pltpu.make_async_remote_copy(
        src_ref=ref, dst_ref=ref, send_sem=send_sem, recv_sem=send_sem, device_id=me, device_id_type=MESH
    ).wait_send()


def arrived(ref, send_sem, recv_sem, me):
    pltpu.make_async_remote_copy(
        src_ref=ref, dst_ref=ref, send_sem=send_sem, recv_sem=recv_sem, device_id=me, device_id_type=MESH
    ).wait_recv()


def iota(shape, dim):
    return lax.broadcasted_iota(jnp.int32, shape, dim).astype(F32)


def panel_kernel(occ_index, vir_index, occ_hbm, vir_hbm, counts_hbm, inter_hbm, win_hbm, out_ref,
                 occ_own, vir_own, counts_ref, idx_own, idx_all, occ_t, vir_t, pick_occ, pick_vir, picked_occ, picked_vir, member, dens_out, dens, charges_out, charges,
                 inter, halves, half_in, pot, win, acc,
                 idx_s, idx_r, occ_s, occ_r, vir_s, vir_r, dens_s, dens_r, int_s, int_r, swap_s, swap_r,
                 ag_s, ag_r, half_s, half_r, ici_s, ici_r, d2d_s, d2d_r, loc):
    y, x, z, k = place()
    me = device(y, x, z, k)
    r = y * 4 + x
    twin = device(y, x, z, 1 - k)
    hops = (
        (0, 1), (1, 0), (0, 3), (3, 0), (1, 1), (3, 3), (1, 3), (3, 1),
        (0, 2), (2, 0), (1, 2), (2, 1), (3, 2), (2, 3), (2, 2),
    )
    plane = [(step(y, dy), step(x, dx)) for dy, dx in hops]
    small = [
        pltpu.make_async_copy(occ_index, occ_own, loc.at[2]),
        pltpu.make_async_copy(vir_index, vir_own, loc.at[3]),
        pltpu.make_async_copy(counts_hbm, counts_ref, loc.at[4]),
    ]
    for copy in small:
        copy.start()
    partners = (
        [device(yy, xx, z, k) for yy, xx in plane]
        + [device(y, x, step(z, d), k) for d in (1, 2, 3)]
        + [twin]
    )
    barrier = pltpu.get_barrier_semaphore()
    for target in partners:
        pl.semaphore_signal(barrier, inc=1, device_id=target, device_id_type=MESH)
    for copy in small:
        copy.wait()
    idx_own[...] = jnp.broadcast_to(jnp.concatenate([occ_own[...], vir_own[...]], axis=1), (8, 128))
    pl.semaphore_wait(barrier, len(partners))
    ups = {"y": device(step(y, 1), x, z, k), "x": device(y, step(x, 1), z, k), "z": device(y, x, step(z, 1), k)}
    downs = {"y": device(step(y, 3), x, z, k), "x": device(y, step(x, 3), z, k), "z": device(y, x, step(z, 3), k)}
    fars = {"y": device(step(y, 2), x, z, k), "x": device(y, step(x, 2), z, k), "z": device(y, x, step(z, 2), k)}
    at = {"y": y, "x": x, "z": z}
    own_cols = pl.ds(pl.multiple_of(r * 128, 128), 128)
    own_inter = pltpu.make_async_copy(inter_hbm, inter.at[z], loc.at[0])
    for copy in (
        pltpu.make_async_copy(idx_own, idx_all.at[r], idx_r.at[0]),
        pltpu.make_async_copy(occ_hbm.at[:, own_cols], occ_t.at[r], occ_r.at[0]),
        pltpu.make_async_copy(vir_hbm.at[:, own_cols], vir_t.at[r], vir_r.at[y]),
        own_inter,
    ):
        copy.start()
    for d, (yy, xx) in enumerate(plane):
        send(idx_own, idx_all.at[r], idx_s.at[0], idx_r.at[0], device(yy, xx, z, k))
    for d, (yy, xx) in enumerate(plane):
        cols = pl.ds(pl.multiple_of((yy * 4 + xx) * 128, 128), 128)
        send(occ_hbm.at[:, cols], occ_t.at[r], occ_s.at[0], occ_r.at[0], device(yy, xx, z, k))
    for d, (yy, xx) in enumerate(plane):
        cols = pl.ds(pl.multiple_of((yy * 4 + xx) * 128, 128), 128)
        send(vir_hbm.at[:, cols], vir_t.at[r], vir_s.at[0], vir_r.at[y], device(yy, xx, z, k))
    send(inter_hbm, inter.at[z], int_s.at[0], int_r.at[0], ups["z"])
    send(inter_hbm, inter.at[z], int_s.at[0], int_r.at[1], downs["z"])
    def load(i, carry):
        cols = pl.ds(pl.multiple_of(i * 128, 128), 128)
        pltpu.make_async_copy(win_hbm.at[:, cols], win.at[i], loc.at[1]).start()
        return carry

    lax.fori_loop(0, 48, load, 0)
    counts = counts_ref[...].astype(F32)
    upper = (iota((768, 768), 0) <= iota((768, 768), 1)).astype(BF)
    ends = jnp.dot(jnp.broadcast_to(counts, (8, 768)).astype(BF), upper, preferred_element_type=F32)[0:1]
    starts = ends - counts

    def members(i, carry):
        basis = iota((256, 768), 0) + (i * 256).astype(F32)
        inside = jnp.logical_and(basis >= starts, basis < ends)
        member[pl.ds(pl.multiple_of(i * 256, 256), 256), :] = jnp.where(inside, 1.0, 0.0).astype(BF)
        return carry

    lax.fori_loop(0, 8, members, 0)
    arrived(idx_all, idx_s.at[0], idx_r.at[0], me)

    def picks(s, carry):
        line = idx_all[s][0:1].astype(F32)
        mine = iota((128, 128), 0) == iota((128, 128), 1)
        column = jnp.sum(jnp.where(mine, jnp.broadcast_to(line, (128, 128)), 0.0), axis=1, keepdims=True)
        rows = pl.ds(pl.multiple_of(s * 64, 64), 64)
        pick_occ[rows, :] = jnp.where(column[0:64] == iota((64, 1024), 1), 1.0, 0.0).astype(BF)
        pick_vir[rows, :] = jnp.where(column[64:128] == iota((64, 2048), 1), 1.0, 0.0).astype(BF)
        return carry

    lax.fori_loop(0, 16, picks, 0)
    arrived(occ_t, occ_s.at[0], occ_r.at[0], me)
    picked_occ[...] = jnp.dot(pick_occ[...], occ_t[...].reshape(1024, 128), preferred_element_type=F32)

    def vir_line(rows, yy):
        cols = pl.ds(pl.multiple_of(yy * 512, 512), 512)
        return jnp.dot(
            pick_vir[rows, cols], vir_t[pl.ds(yy * 4, 4)].reshape(512, 128), preferred_element_type=F32
        )

    for i, dy in enumerate((0, 3, 1, 2)):
        yy = step(y, dy)
        arrived(vir_t.at[pl.ds(yy * 4, 4)], vir_s.at[0], vir_r.at[yy], me)
        if i == 0:
            picked_vir[...] = vir_line(slice(None), yy)
        elif i < 3:
            picked_vir[...] += vir_line(slice(None), yy)
    for dy in (2, 1, 3, 0):
        yy = step(y, dy)
        rows = pl.ds(pl.multiple_of(yy * 256, 256), 256)
        second_rows = picked_vir[rows, :] + vir_line(rows, step(y, 2))
        dens_out[pl.ds(yy * 4, 4)] = (picked_occ[rows, :] * second_rows).astype(BF).reshape(4, 64, 128)
        for dx in (2, 1, 3, 0):
            xx = step(x, dx)
            other = yy * 4 + xx
            if dy == 0 and dx == 0:
                pltpu.make_async_copy(dens_out.at[r], dens.at[r], dens_r.at[0]).start()
            else:
                send(dens_out.at[other], dens.at[r], dens_s.at[0], dens_r.at[0], device(yy, xx, z, k))

    left(idx_all.at[pl.ds(0, 15)], idx_s.at[0], me)
    left(occ_t.at[pl.ds(0, 15)], occ_s.at[0], me)
    left(vir_t.at[pl.ds(0, 15)], vir_s.at[0], me)
    arrived(dens, dens_s.at[0], dens_r.at[0], me)
    density = jnp.concatenate([dens[s] for s in range(16)], axis=1)
    own_charges = jnp.dot(density, member[...], preferred_element_type=F32).astype(BF)
    charges_out[...] = own_charges.reshape(4, 16, 768)
    charges[y, x, z] = charges_out[z]
    for d in (1, 2, 3):
        zz = step(z, d)
        send(charges_out.at[zz], charges.at[y, x, z], swap_s.at[0], swap_r.at[0], device(y, x, zz, k))
    below, above = step(z, 3), step(z, 1)
    arrived(inter.at[below], int_s.at[0], int_r.at[0], me)
    top, bottom = pl.ds(0, 384), pl.ds(384, 384)
    send(inter.at[below, top], inter.at[below, top], int_s.at[0], int_r.at[2], ups["z"])
    arrived(inter.at[above], int_s.at[0], int_r.at[1], me)
    send(inter.at[above, bottom], inter.at[above, bottom], int_s.at[0], int_r.at[3], downs["z"])
    left(dens.at[pl.ds(0, 15)], dens_s.at[0], me)
    arrived(charges_out.at[pl.ds(0, 3)], swap_s.at[0], swap_r.at[0], me)
    views = (
        lambda a, b, h=None: charges.at[b, a, pl.ds(0, 2)],
        lambda a, b, h=None: charges.at[a, b, pl.ds(2, 2)],
    )
    axes = (("x", "y"), ("y", "x"))

    def plane_sems(part, i):
        return ag_s.at[0], ag_r.at[part, i]

    def plane_block(part, a, b):
        return views[part](step(at[axes[part][0]], a), step(at[axes[part][1]], b))

    def plane_second(part, a):
        ref = plane_block(part, a, 0)
        send(ref, ref, *plane_sems(part, 3 + a), ups[axes[part][1]])
        send(ref, ref, *plane_sems(part, 7 + a), downs[axes[part][1]])

    def plane_first_arrival(part, a):
        arrived(plane_block(part, a, 0), *plane_sems(part, {3: 0, 1: 1, 2: 2}[a]), me)
        plane_second(part, a)

    def plane_second_arrival(part, a):
        ref = plane_block(part, a, 3)
        arrived(ref, *plane_sems(part, 3 + a), me)
        if a in (0, 2):
            send(ref, ref, *plane_sems(part, 11), ups[axes[part][1]])
        ref = plane_block(part, a, 1)
        arrived(ref, *plane_sems(part, 7 + a), me)
        if a in (1, 3):
            send(ref, ref, *plane_sems(part, 11), downs[axes[part][1]])

    for part in range(2):
        ref = plane_block(part, 0, 0)
        send(ref, ref, *plane_sems(part, 0), ups[axes[part][0]])
        send(ref, ref, *plane_sems(part, 1), downs[axes[part][0]])
        send(ref, ref, *plane_sems(part, 2), fars[axes[part][0]])
    for part in range(2):
        plane_second(part, 0)
    for what, a in ((1, 3), (1, 1), (2, 0), (1, 2), (2, 3), (2, 1), (2, 2)):
        for part in range(2):
            (plane_first_arrival if what == 1 else plane_second_arrival)(part, a)
    left(charges_out.at[pl.ds(0, 3)], swap_s.at[0], me)
    arrived(charges.at[step(y, 2), :, pl.ds(0, 2)], *plane_sems(0, 11), me)
    arrived(charges.at[:, step(x, 2), pl.ds(2, 2)], *plane_sems(1, 11), me)
    own_inter.wait()
    arrived(inter.at[step(z, 2), top], int_s.at[0], int_r.at[2], me)
    arrived(inter.at[step(z, 2), bottom], int_s.at[0], int_r.at[3], me)

    lhs = jnp.concatenate([charges[:, :, zz].reshape(256, 768) for zz in range(4)], axis=1)
    halves[...] = jnp.dot(lhs, inter[...].reshape(3072, 384), preferred_element_type=F32).reshape(2, 128, 384)
    send(halves.at[1 - k], half_in, half_s.at[0], half_r.at[0], twin)
    left(inter.at[pl.ds(0, 3)], int_s.at[0], me)
    left(pot.at[0, pl.ds(0, 3), pl.ds(0, 3), pl.ds(0, 640)], ag_s.at[0], me)
    arrived(half_in, half_s.at[0], half_r.at[0], me)
    total = (halves[k] + half_in[...]).astype(BF)

    def rows(s, kk=k, n=128):
        return pl.ds(pl.multiple_of(kk * 512 + s * 128, 128), n)

    def half_rows(kk=k):
        return pl.ds(pl.multiple_of(kk * 512, 512), 512)

    for j in range(3):
        pot[j, y, x, rows(z), :] = total[:, 128 * j:128 * j + 128]
    orders = ("zyx", "xzy", "yxz")
    first = (
        lambda s: pot.at[0, y, x, rows(s)],
        lambda s: pot.at[1, y, s, rows(z)],
        lambda s: pot.at[2, s, x, rows(z)],
    )

    def two(h):
        return slice(None) if h is None else pl.ds(2 * h, 2)

    second = (
        lambda s, h=None, kk=k: pot.at[0, s, x, half_rows(kk) if h is None else pl.ds(pl.multiple_of(kk * 512 + 256 * h, 256), 256)],
        lambda s, h=None, kk=k: pot.at[1, y, two(h), rows(s, kk)],
        lambda s, h=None, kk=k: pot.at[2, two(h), s, rows(z, kk)],
    )
    third = (
        lambda s, q, kk=k: pot.at[0, q, s, half_rows(kk)],
        lambda s, q, kk=k: pot.at[1, s, :, rows(q, kk)],
        lambda s, q, kk=k: pot.at[2, :, q, rows(s, kk)],
    )

    def ici(j, i):
        return ici_s.at[0], ici_r.at[j, i]

    def share(j, ref, group):
        send(ref, ref, d2d_s.at[0], d2d_r.at[j, group], twin)

    def shared(j, group, ref):
        arrived(ref, d2d_s.at[0], d2d_r.at[j, group], me)

    def chunk_group(a, b):
        return 1 + (a in (1, 2)) + 2 * (b == 2)

    c1, c2, c3 = ([at[orders[j][level]] for j in range(3)] for level in range(3))

    def third_send(j, a):
        ref = third[j](c3[j], step(c2[j], a))
        send(ref, ref, *ici(j, 7 + a), ups[orders[j][2]])
        send(ref, ref, *ici(j, 11 + a), downs[orders[j][2]])

    def third_arrival(a):
        for j in range(3):
            q = step(c2[j], a)
            ref = third[j](step(c3[j], 3), q)
            arrived(ref, *ici(j, 7 + a), me)
            if a in (0, 2):
                send(ref, ref, *ici(j, 15 + a), ups[orders[j][2]])
            share(j, ref, chunk_group(a, 3))
            ref = third[j](step(c3[j], 1), q)
            arrived(ref, *ici(j, 11 + a), me)
            if a in (1, 3):
                send(ref, ref, *ici(j, 15 + a), downs[orders[j][2]])
            share(j, ref, chunk_group(a, 1))

    def far_arrival(a):
        for j in range(3):
            ref = third[j](step(c3[j], 2), step(c2[j], a))
            arrived(ref, *ici(j, 15 + a), me)
            share(j, ref, chunk_group(a, 2))

    for j in range(3):
        ref = first[j](c1[j])
        send(ref, ref, *ici(j, 0), ups[orders[j][0]])
        send(ref, ref, *ici(j, 0), downs[orders[j][0]])
        send(ref, ref, *ici(j, 0), fars[orders[j][0]])
    pltpu.make_async_copy(win, win, loc.at[1]).wait()
    for j in range(3):
        arrived(pot.at[j, pl.ds(0, 3), 0, pl.ds(0, 128)], *ici(j, 0), me)
        ref = second[j](c2[j])
        send(ref, ref, *ici(j, 3), ups[orders[j][1]])
        send(ref, ref, *ici(j, 4), downs[orders[j][1]])
        third_send(j, 0)
        share(j, ref, 0)
    for j in range(3):
        ref = second[j](step(c2[j], 3))
        arrived(ref, *ici(j, 3), me)
        half = second[j](step(c2[j], 3), 0)
        send(half, half, *ici(j, 5), ups[orders[j][1]])
        third_send(j, 3)
        share(j, ref, 0)
        ref = second[j](step(c2[j], 1))
        arrived(ref, *ici(j, 4), me)
        half = second[j](step(c2[j], 1), 1)
        send(half, half, *ici(j, 6), downs[orders[j][1]])
        third_send(j, 1)
        share(j, ref, 0)
    third_arrival(0)
    for j in range(3):
        far = step(c2[j], 2)
        arrived(second[j](far, 0), *ici(j, 5), me)
        arrived(second[j](far, 1), *ici(j, 6), me)
        third_send(j, 2)
        share(j, second[j](far), 0)

    started = [False]

    def add(points, row_starts, size, last=False):
        lhs = jnp.concatenate([
            jnp.concatenate([pot[j, yy, xx, pl.ds(pl.multiple_of(s, 128), size), :] for s in row_starts], axis=0)
            for j, yy, xx in points], axis=1)
        rhs = jnp.concatenate([win[(yy * 4 + xx) * 3 + j] for j, yy, xx in points], axis=1)
        value = lax.dot_general(lhs, rhs, (((1,), (1,)), ((), ())), preferred_element_type=F32)
        if not started[0]:
            acc[...] = value
            started[0] = True
            return
        if last:
            value = (value + acc[...]).astype(BF)
            for kk in range(2):
                for zz in range(4):
                    for i in range(8):
                        here, there = kk * 512 + zz * 128 + i * 16, (kk * 8 + i) * 64 + zz * 16
                        out_ref[there:there + 16] = value[here:here + 16]
            return
        for i, s in enumerate(row_starts):
            where = pl.ds(pl.multiple_of(s, 128), size)
            acc[where, :] += value[i * size:(i + 1) * size]

    def both(s):
        return [s * 128, 512 + s * 128]

    def add_second(j):
        shared(j, 0, pot.at[j, :, 0, pl.ds(0, 512)])
        if j == 0:
            add([(0, q, x) for q in range(4)], [0], 1024)
        if j == 1:
            add([(1, y, q) for q in range(4)], [0], 1024)
        if j == 2:
            add([(2, a, b) for a in range(4) for b in range(4)], both(z), 128)

    def add_third(j, chunk_pair, others, last=False):
        shared(j, chunk_group(chunk_pair[0], others[0]), pot.at[j, pl.ds(0, 2 * len(others)), 0, pl.ds(0, 512)])
        qs = [step(c2[j], a) for a in chunk_pair]
        ss = [step(c3[j], b) for b in others]
        if j == 0:
            add([(0, q, s) for q in qs for s in ss], [0], 1024, last)
        if j == 1:
            add([(1, s, b) for s in ss for b in range(4)], both(qs[0]) + both(qs[1]), 128)
        if j == 2:
            add([(2, a, q) for a in range(4) for q in qs], [v for s in ss for v in both(s)], 128)

    third_arrival(3)
    add_second(0)
    add_second(1)
    third_arrival(1)
    add_second(2)
    add_third(0, (0, 3), (3, 1))
    third_arrival(2)
    add_third(1, (0, 3), (3, 1))
    add_third(2, (0, 3), (3, 1))
    add_third(0, (1, 2), (3, 1))
    far_arrival(0)
    add_third(1, (1, 2), (3, 1))
    far_arrival(3)
    add_third(2, (1, 2), (3, 1))
    far_arrival(1)
    add_third(0, (0, 3), (2,))
    far_arrival(2)
    add_third(1, (0, 3), (2,))
    add_third(2, (0, 3), (2,))
    for j in (1, 2, 0):
        add_third(j, (1, 2), (2,), j == 0)
    left(halves.at[1 - k], half_s.at[0], me)
    left(pot.at[:, :, :, half_rows()], d2d_s.at[0], me)
    left(pot.at[:, pl.ds(0, 3), pl.ds(0, 3), pl.ds(0, 896)], ici_s.at[0], me)


def mask_kernel(least, coupling, out_ref):
    shape = out_ref.shape
    ahead = lax.broadcasted_iota(jnp.int32, shape, 1) - lax.broadcasted_iota(jnp.int32, shape, 0)
    value = coupling[...].astype(F32)
    keep = ahead >= least[0] + pl.program_id(0) * shape[0]
    out_ref[...] = jnp.where(keep, value, jnp.zeros_like(value)).astype(BF)


def sems(*shape):
    return pltpu.SemaphoreType.DMA(shape)


ANY = pl.BlockSpec(memory_space=pl.ANY)
VMEM = pl.BlockSpec(memory_space=pltpu.VMEM)


def shards(
    occ_coef, vir_coef, atom_counts, occ_index, vir_index, interaction, window_charges, panel_start
):
    coupling = pl.pallas_call(
        panel_kernel,
        out_shape=jax.ShapeDtypeStruct((1024, 1024), BF),
        in_specs=[ANY] * 7,
        out_specs=VMEM,
        scratch_shapes=[
            pltpu.VMEM((1, 64), jnp.int32),
            pltpu.VMEM((1, 64), jnp.int32),
            pltpu.VMEM((1, 768), jnp.int32),
            pltpu.VMEM((8, 128), jnp.int32),
            pltpu.VMEM((16, 8, 128), jnp.int32),
            pltpu.VMEM((16, 64, 128), BF),
            pltpu.VMEM((16, 128, 128), BF),
            pltpu.VMEM((1024, 1024), BF),
            pltpu.VMEM((1024, 2048), BF),
            pltpu.VMEM((1024, 128), F32),
            pltpu.VMEM((1024, 128), F32),
            pltpu.VMEM((2048, 768), BF),
            pltpu.VMEM((16, 64, 128), BF),
            pltpu.VMEM((16, 64, 128), BF),
            pltpu.VMEM((4, 16, 768), BF),
            pltpu.VMEM((4, 4, 4, 16, 768), BF),
            pltpu.VMEM((4, 768, 384), BF),
            pltpu.VMEM((2, 128, 384), F32),
            pltpu.VMEM((128, 384), F32),
            pltpu.VMEM((3, 4, 4, 1024, 128), BF),
            pltpu.VMEM((48, 1024, 128), BF),
            pltpu.VMEM((1024, 1024), F32),
            sems(1), sems(1), sems(1), sems(1), sems(1), sems(4), sems(1), sems(1),
            sems(1), sems(4), sems(1), sems(1), sems(1), sems(2, 12), sems(1), sems(1),
            sems(1), sems(3, 19), sems(1), sems(3, 5), sems(5),
        ],
        compiler_params=pltpu.CompilerParams(
            collective_id=0, has_side_effects=True, vmem_limit_bytes=60 * 2**20
        ),
    )(occ_index[None], vir_index[None], occ_coef, vir_coef, atom_counts, interaction, window_charges)
    least = panel_start - lax.axis_index(("row", "col")) * window_charges.shape[0]
    return pl.pallas_call(
        mask_kernel,
        grid=(2,),
        out_shape=jax.ShapeDtypeStruct((1024, 1024), BF),
        in_specs=[pl.BlockSpec(memory_space=pltpu.SMEM), pl.BlockSpec((512, 1024), lambda i: (i, 0))],
        out_specs=pl.BlockSpec((512, 1024), lambda i: (i, 0)),
    )(least, coupling)


def solution(mesh):
    placed = (
        P("row", "col"),
        P("row", "col"),
        P("col", None),
        P("row"),
        P("row"),
        P("col", "row"),
        P(("row", "col"), None),
        P(),
    )
    return jax.shard_map(
        shards, mesh=mesh, in_specs=placed, out_specs=P(None, ("row", "col")), check_vma=False
    )
```
